256 devices in a mesh: group: 4 (over x_hi, core), blk: 64 (over y, x_lo, z).
Axes of the slice: x: 4 (x_hi: 2, x_lo: 2; x = x_hi * 2 + x_lo), y: 4, z: 8, core: 2. Of those that a mesh axis runs over, the one named last changes fastest.
Arguments:
- images: bfloat16 [16384, 1152], P(('group', 'blk')), may hold values from -0.72 to 0.72
- texts: bfloat16 [16384, 1152], P(('group', 'blk')), may hold values from -0.72 to 0.72
- logit_scale: float32 [1], replicated, may hold values from 3 to 8
- bias: float32 [1], replicated, may hold values from -3 to -1
Outputs:
- image_grads: float32 [16384, 1152], P(('group', 'blk'))
- text_grads: float32 [16384, 1152], P(('group', 'blk'))
The draws below stay inside these ranges and needn't reach their ends.
All inputs are finite; a program needn't handle non-finite values.
Results may differ from the reference program's by a relative error of at most 0.00067.
Values may be sent and summed in bfloat16 or wider, within the bound.
No kernel may reach another device: no remote copies, remote signals or barrier semaphores. Data moves between devices by JAX's collectives and lax.ppermute only.
A program may use at most 128 MiB of HBM per device.

```python
import math
import jax
import jax.numpy as jnp
from jax import lax

D = 1152
ROWS = 16384


cluster_total = 64


def shared_base(key):
    pick_key, center_key, own_key = jax.random.split(key, 3)
    labels = jax.random.randint(pick_key, (ROWS,), 0, cluster_total)
    centers = jax.random.normal(center_key, (cluster_total, D), jnp.float32)
    own = jax.random.normal(own_key, (ROWS, D), jnp.float32)
    return 0.6 * centers[labels] + 0.75 * own


def row_scaled(key, base):
    row_scale = jnp.exp(jax.random.uniform(key, (base.shape[0], 1), jnp.float32, math.log(0.3), math.log(3.0)))
    return 0.06 * jnp.clip(base, -4.0, 4.0) * row_scale


def draw_images(key, part):
    base = shared_base(key)
    key = jax.random.fold_in(key, 11)
    return row_scaled(key, base).astype(jnp.bfloat16)


def draw_texts(key, part):
    base = shared_base(key)
    key = jax.random.fold_in(key, 23)
    noise_key, scale_key = jax.random.split(key)
    noise = jax.random.normal(noise_key, (ROWS, D), jnp.float32)
    return row_scaled(scale_key, 0.8 * base + 0.6 * noise).astype(jnp.bfloat16)


def setup_inputs(seed: int = 0) -> dict:
    key_list = jax.random.split(jax.random.key(seed), 5)
    images = draw_images(jax.random.fold_in(key_list[4], 71), 0)
    texts = draw_texts(jax.random.fold_in(key_list[4], 71), 0)
    logit_scale = jnp.clip(jnp.exp(jax.random.uniform(key_list[2], (1,), jnp.float32, math.log(3.0), math.log(8.0))), 3.0, 8.0)
    bias = jnp.clip(jax.random.uniform(key_list[3], (1,), jnp.float32, -3.0, -1.0), -3.0, -1.0)
    return {"images": images, "texts": texts, "logit_scale": logit_scale, "bias": bias}


epsilon = 1e-06

def normalize(embedding):
    values = embedding.astype(jnp.float32)
    inverse = lax.rsqrt(lax.optimization_barrier(jnp.sum(values * values, axis=-1, keepdims=True)) + epsilon)
    return (values * inverse, inverse)

def unit_grad(unit_vec, inverse, grad_sum):
    return (grad_sum - unit_vec * lax.optimization_barrier(jnp.sum(unit_vec * grad_sum, axis=-1, keepdims=True))) * inverse

def reference(images, texts, logit_scale, bias):
    image_unit, image_inv = normalize(images)
    text_unit, text_inv = normalize(texts)
    image_low = lax.optimization_barrier(image_unit.astype(jnp.bfloat16)).astype(jnp.float32)
    text_low = lax.optimization_barrier(text_unit.astype(jnp.bfloat16)).astype(jnp.float32)
    factor = logit_scale[0]
    offset = bias[0]
    span_rows = math.gcd(ROWS, 1024)
    num_blocks = ROWS // span_rows
    image_ids = jnp.arange(ROWS, dtype=jnp.int32)
    blocks = text_low.reshape(num_blocks, span_rows, D)
    starts = jnp.arange(num_blocks, dtype=jnp.int32) * span_rows

    def visit(image_sum, inputs):
        text_block, row_from = inputs
        logits = factor * lax.dot_general(text_block, image_low, (((1,), (1,)), ((), ())), precision=lax.Precision.HIGHEST) + offset
        text_ids = row_from + jnp.arange(span_rows, dtype=jnp.int32)
        positive = (text_ids[:, None] == image_ids[None, :]).astype(jnp.float32)
        weights_tile = (factor * (jax.nn.sigmoid(logits) - positive)).astype(jnp.bfloat16)
        weights_tile = lax.optimization_barrier(weights_tile).astype(jnp.float32)
        text_part = jnp.dot(weights_tile, image_low, precision=lax.Precision.HIGHEST)
        image_sum = image_sum + lax.dot_general(weights_tile, text_block, (((0,), (0,)), ((), ())), precision=lax.Precision.HIGHEST)
        return (image_sum, text_part)
    image_sum, text_parts = lax.scan(visit, jnp.zeros((ROWS, D), jnp.float32), (blocks, starts))
    text_sum = text_parts.reshape(ROWS, D)
    return (unit_grad(image_unit, image_inv, image_sum), unit_grad(text_unit, text_inv, text_sum))
```

```python
import jax
import jax.numpy as jnp
import numpy as np
from jax import lax
from jax.sharding import PartitionSpec as P

epsilon = 1e-06

SHAPE = (2, 2, 4, 2, 8)
AXES = ("group", "blk")
SHRINK = 0.25


def neighbour_pairs(axis, phase):
    perm = []
    for i, (xh, core, y, xl, z) in enumerate(np.ndindex(*SHAPE)):
        at = {"x": 2 * xh + xl, "y": y, "z": z}
        n = {"x": 4, "y": 4, "z": 8}[axis]
        p = at[axis]
        if (phase + core) % 2 == 0:
            at[axis] = p ^ 1
        else:
            at[axis] = (p + 1) % n if p % 2 else (p - 1) % n
        there = (at["x"] // 2, core, at["y"], at["x"] % 2, at["z"])
        perm.append((i, int(np.ravel_multi_index(there, SHAPE))))
    return perm


PX, PY, PZ = ([neighbour_pairs(axis, 0), neighbour_pairs(axis, 1)] for axis in "xyz")
PC = [(i, i ^ 64) for i in range(256)]


def swap(array, perm):
    return lax.ppermute(array, AXES, perm)


def join(*arrays):
    return jnp.concatenate(arrays, axis=0)


def normalize(embedding):
    values = embedding.astype(jnp.float32)
    inverse = lax.rsqrt(jnp.sum(values * values, axis=-1, keepdims=True) + epsilon)
    return (values * inverse, inverse)


def unit_grad(unit_vec, inverse, grad_sum):
    return (grad_sum - unit_vec * jnp.sum(unit_vec * grad_sum, axis=-1, keepdims=True)) * inverse


def gather_doubling(own, perms):
    held = own
    for perm in perms:
        held = join(held, swap(held, perm))
    return held


def gather_z(own):
    first = join(own, swap(own, PZ[0]))
    second = swap(first, PZ[1])
    third = swap(second, PZ[0])
    fourth = swap(third, PZ[1])
    return join(first, second, third, fourth)


def send_sum(part, perm):
    return swap((part * SHRINK).astype(jnp.float16), perm).astype(jnp.float32) * (1 / SHRINK)


def scatter_doubling(total, perms):
    for perm in reversed(perms):
        n = total.shape[0] // 2
        total = total[:n] + send_sum(total[n:], perm)
    return total


def scatter_z(total):
    n = total.shape[0] // 4
    first, second, third, fourth = (total[i * n : (i + 1) * n] for i in range(4))
    third = third + send_sum(fourth, PZ[1])
    second = second + send_sum(third, PZ[0])
    first = first + send_sum(second, PZ[1])
    return first[: n // 2] + send_sum(first[n // 2 :], PZ[0])


def body(images, texts, logit_scale, bias):
    image_unit, image_inv = normalize(images)
    text_unit, text_inv = normalize(texts)
    image_low = image_unit.astype(jnp.bfloat16)
    text_low = text_unit.astype(jnp.bfloat16)
    factor = logit_scale[0]
    offset = bias[0]
    rows = images.shape[0]
    half = rows // 2
    images_a = gather_doubling(image_low[:half], PX + PY)
    images_b = gather_doubling(image_low[half:], PY + PX)
    texts_core = gather_z(text_low)
    texts_other = swap(texts_core, PC)
    image_all = join(images_a, images_b)
    text_all = join(texts_core, texts_other)
    logits = (
        factor
        * lax.dot_general(
            text_all, image_all, (((1,), (1,)), ((), ())), preferred_element_type=jnp.float32
        )
        + offset
    )
    n = image_all.shape[0]
    row = lax.broadcasted_iota(jnp.int32, (n, n), 0)
    col = lax.broadcasted_iota(jnp.int32, (n, n), 1)
    image_id = jnp.where(
        col < half, col, jnp.where((col >= n // 2) & (col < n // 2 + half), col - n // 2 + half, n)
    )
    positive = (row == image_id).astype(jnp.float32)
    weights = (factor * (jax.nn.sigmoid(logits) - positive)).astype(jnp.bfloat16)
    text_sum = jnp.dot(weights, image_all, preferred_element_type=jnp.float32)
    image_sum = lax.dot_general(
        weights, text_all, (((0,), (0,)), ((), ())), preferred_element_type=jnp.float32
    )
    image_own = join(
        scatter_doubling(image_sum[: n // 2], PX + PY), scatter_doubling(image_sum[n // 2 :], PY + PX)
    )
    text_core = text_sum[: n // 2] + swap(text_sum[n // 2 :], PC)
    text_own = scatter_z(text_core)
    return (unit_grad(image_unit, image_inv, image_own), unit_grad(text_unit, text_inv, text_own))


def solution(mesh):
    return jax.shard_map(
        body,
        mesh=mesh,
        in_specs=(P(("group", "blk"), None), P(("group", "blk"), None), P(), P()),
        out_specs=(P(("group", "blk"), None), P(("group", "blk"), None)),
        check_vma=False,
    )
```

```python
import jax
import jax.numpy as jnp
import numpy as np
from jax import lax
from jax.sharding import PartitionSpec as P

epsilon = 1e-06

SHAPE = (2, 2, 4, 2, 8)
AXES = ("group", "blk")
SHRINK = 0.25


def neighbour_pairs(axis, phase):
    perm = []
    for i, (xh, core, y, xl, z) in enumerate(np.ndindex(*SHAPE)):
        at = {"x": 2 * xh + xl, "y": y, "z": z}
        n = {"x": 4, "y": 4, "z": 8}[axis]
        p = at[axis]
        if (phase + core) % 2 == 0:
            at[axis] = p ^ 1
        else:
            at[axis] = (p + 1) % n if p % 2 else (p - 1) % n
        there = (at["x"] // 2, core, at["y"], at["x"] % 2, at["z"])
        perm.append((i, int(np.ravel_multi_index(there, SHAPE))))
    return perm


PX, PY, PZ = ([neighbour_pairs(axis, 0), neighbour_pairs(axis, 1)] for axis in "xyz")
PC = [(i, i ^ 64) for i in range(256)]


def swap(array, perm):
    return lax.ppermute(array, AXES, perm)


def join(*arrays):
    return jnp.concatenate(arrays, axis=0)


def normalize(embedding):
    values = embedding.astype(jnp.float32)
    inverse = lax.rsqrt(jnp.sum(values * values, axis=-1, keepdims=True) + epsilon)
    return (values * inverse, inverse)


def unit_grad(unit_vec, inverse, grad_sum):
    return (grad_sum - unit_vec * jnp.sum(unit_vec * grad_sum, axis=-1, keepdims=True)) * inverse


def step(*arrays):
    return lax.optimization_barrier(arrays)


def gather(images, texts):
    half = images.shape[0] // 2
    a, b, text_parts = images[:half], images[half:], [texts]
    for k, (pa, pb) in enumerate(zip(PX + PY, PY + PX)):
        text = join(*text_parts) if k < 2 else text_parts[-1]
        got_text, got_a, got_b = step(swap(text, PZ[k % 2]), swap(a, pa), swap(b, pb))
        a, b = join(a, got_a), join(b, got_b)
        text_parts.append(got_text)
    return a, b, join(*text_parts)


def shrunk(part):
    return (part * SHRINK).astype(jnp.float16)


def grown(part):
    return part.astype(jnp.float32) * (1 / SHRINK)


def scatter(a, b, text):
    n = text.shape[0] // 4
    texts = [text[i * n : (i + 1) * n] for i in range(4)]
    half_text = n // 2
    for k, (pa, pb) in reversed(list(enumerate(zip(PX + PY, PY + PX)))):
        n = a.shape[0] // 2
        out_text = texts[k] if k else texts[0][half_text:]
        got_a, got_b, got_text = step(
            swap(shrunk(a[n:]), pa), swap(shrunk(b[n:]), pb), swap(shrunk(out_text), PZ[k % 2])
        )
        a, b = a[:n] + grown(got_a), b[:n] + grown(got_b)
        if k:
            texts[k - 1] = texts[k - 1] + grown(got_text)
        else:
            texts[0] = texts[0][:half_text] + grown(got_text)
    return a, b, texts[0]


def logits_of(texts, images, factor, offset):
    product = lax.dot_general(
        texts, images, (((1,), (1,)), ((), ())), preferred_element_type=jnp.float32
    )
    return factor * product + offset


def body(images, texts, logit_scale, bias):
    image_unit, image_inv = normalize(images)
    text_unit, text_inv = normalize(texts)
    image_low = image_unit.astype(jnp.bfloat16)
    text_low = text_unit.astype(jnp.bfloat16)
    factor = logit_scale[0]
    offset = bias[0]
    rows = images.shape[0]
    half = rows // 2
    images_a, images_b, texts_core = gather(image_low, text_low)
    texts_other = swap(texts_core, PC)
    image_all = join(images_a, images_b)
    n = image_all.shape[0]
    row = lax.broadcasted_iota(jnp.int32, (n // 2, n), 0)
    col = lax.broadcasted_iota(jnp.int32, (n // 2, n), 1)
    image_id = jnp.where(
        col < half, col, jnp.where((col >= n // 2) & (col < n // 2 + half), col - n // 2 + half, n)
    )
    positive = (row == image_id).astype(jnp.float32)
    weights_core = (
        factor * (jax.nn.sigmoid(logits_of(texts_core, image_all, factor, offset)) - positive)
    ).astype(jnp.bfloat16)
    texts_other, weights_core = lax.optimization_barrier((texts_other, weights_core))
    weights_other = (
        factor * jax.nn.sigmoid(logits_of(texts_other, image_all, factor, offset))
    ).astype(jnp.bfloat16)
    text_sum_other = jnp.dot(weights_other, image_all, preferred_element_type=jnp.float32)
    weights_other, text_sum_other = lax.optimization_barrier((weights_other, text_sum_other))
    got_text = swap(text_sum_other, PC)
    weights = join(weights_core, weights_other)
    image_sum = lax.dot_general(
        weights,
        join(texts_core, texts_other),
        (((0,), (0,)), ((), ())),
        preferred_element_type=jnp.float32,
    )
    weights_core, image_sum = lax.optimization_barrier((weights_core, image_sum))
    text_sum_core = jnp.dot(weights_core, image_all, preferred_element_type=jnp.float32)
    a, b, text_own = scatter(image_sum[: n // 2], image_sum[n // 2 :], text_sum_core + got_text)
    return (
        unit_grad(image_unit, image_inv, join(a, b)),
        unit_grad(text_unit, text_inv, text_own),
    )


def solution(mesh):
    return jax.shard_map(
        body,
        mesh=mesh,
        in_specs=(P(("group", "blk"), None), P(("group", "blk"), None), P(), P()),
        out_specs=(P(("group", "blk"), None), P(("group", "blk"), None)),
        check_vma=False,
    )
```

```python
import jax
import jax.numpy as jnp
import numpy as np
from jax import lax
from jax.experimental import pallas as pl
from jax.experimental.pallas import tpu as pltpu
from jax.sharding import PartitionSpec as P

epsilon = 1e-06

SHAPE = (2, 2, 4, 2, 8)
AXES = ("group", "blk")
SHRINK = 0.25
SMALL = pltpu.CompilerParams(vmem_limit_bytes=4 * 2**20)


def neighbour_pairs(axis, phase):
    perm = []
    for i, (xh, core, y, xl, z) in enumerate(np.ndindex(*SHAPE)):
        at = {"x": 2 * xh + xl, "y": y, "z": z}
        n = {"x": 4, "y": 4, "z": 8}[axis]
        p = at[axis]
        if (phase + core) % 2 == 0:
            at[axis] = p ^ 1
        else:
            at[axis] = (p + 1) % n if p % 2 else (p - 1) % n
        there = (at["x"] // 2, core, at["y"], at["x"] % 2, at["z"])
        perm.append((i, int(np.ravel_multi_index(there, SHAPE))))
    return perm


PX, PY, PZ = ([neighbour_pairs(axis, 0), neighbour_pairs(axis, 1)] for axis in "xyz")
PC = [(i, i ^ 64) for i in range(256)]


def swap(array, perm):
    return lax.ppermute(array, AXES, perm)


def join(*arrays):
    return jnp.concatenate(arrays, axis=0)


def step(*arrays):
    return lax.optimization_barrier(arrays)


def unit_of(embedding):
    values = embedding.astype(jnp.float32)
    inverse = lax.rsqrt(jnp.sum(values * values, axis=-1, keepdims=True) + epsilon)
    return values * inverse, inverse


def low_kernel(rows, low):
    low[...] = unit_of(rows[...])[0].astype(jnp.bfloat16)


def low_rows(rows):
    out = jax.ShapeDtypeStruct(rows.shape, jnp.bfloat16)
    return pl.pallas_call(low_kernel, out_shape=out, compiler_params=SMALL)(rows)


def shrunk(part):
    return (part * SHRINK).astype(jnp.float16)


def grown(part):
    return part.astype(jnp.float32) * (1 / SHRINK)


def grads_kernel(images, texts, image_sum, text_sum, image_out, text_out):
    for rows, summed, out in ((images, image_sum, image_out), (texts, text_sum, text_out)):
        unit, inverse = unit_of(rows[...])
        total = summed[...]
        along = jnp.sum(unit * total, axis=-1, keepdims=True)
        out[...] = (total - unit * along) * inverse


def grads(images, texts, *sums):
    out = jax.ShapeDtypeStruct(images.shape, jnp.float32)
    return pl.pallas_call(grads_kernel, out_shape=(out, out), compiler_params=SMALL)(
        images, texts, *sums
    )


def weights_of(texts, images, factor, offset, own=None):
    product = lax.dot_general(
        texts, images, (((1,), (1,)), ((), ())), preferred_element_type=jnp.float32
    )
    value = jax.nn.sigmoid(factor * product + offset)
    if own is not None:
        row = lax.broadcasted_iota(jnp.int32, value.shape, 0)
        col = lax.broadcasted_iota(jnp.int32, value.shape, 1)
        half, cols = own // 2, value.shape[1] // 2
        image = jnp.where(col < cols, col, col - cols + half)
        mine = (jnp.where(col < cols, col, col - cols) < half) & (row == image)
        value = value - mine.astype(jnp.float32)
    return (factor * value).astype(jnp.bfloat16)


def dot(a, b):
    return jnp.dot(a, b, preferred_element_type=jnp.float32)


def dot_t(a, b):
    return lax.dot_general(a, b, (((0,), (0,)), ((), ())), preferred_element_type=jnp.float32)


def body(images, texts, logit_scale, bias):
    factor = logit_scale[0]
    offset = bias[0]
    n = images.shape[0]
    text_low, image_low = low_rows(texts), low_rows(images)

    h = n // 2
    a, b = image_low[:h], image_low[h:]
    parts = [text_low]
    for k, (pa, pb) in enumerate(zip(PX + PY, PY + PX)):
        t = join(*parts) if k < 2 else parts[-1]
        if k == 2:
            own_a = join(*parts)
            other_a = swap(own_a, PC)
        if k == 3:
            first = join(a, b)
            own_0 = join(own_a, parts[3])
        if k < 3:
            got_t, got_a, got_b = step(swap(t, PZ[k % 2]), swap(a, pa), swap(b, pb))
        else:
            got_a, got_b, got_t = step(swap(a, pa), swap(b, pb), swap(t, PZ[k % 2]))
        parts.append(got_t)
        if k < 3:
            a, b = join(a, got_a), join(b, got_b)

    first_own_0 = weights_of(own_0, first, factor, offset, n)
    first_other_a = weights_of(other_a, first, factor, offset)
    text_own_0 = dot(first_own_0, first)
    text_other_a = dot(first_other_a, first)
    sum_first = dot_t(first_own_0, own_0) + dot_t(first_other_a, other_a)

    h, m, q = 4 * n, 2 * n, 6 * n
    second = join(got_a, got_b)
    own_1 = parts[4]
    other_b = swap(join(parts[3], own_1), PC)
    own = join(own_0, own_1)
    second_own = weights_of(own, second, factor, offset)
    sum_second = dot_t(second_own, own)
    sum_second, second_own, other_b, other_a, text_other_a = lax.optimization_barrier(
        (sum_second, second_own, other_b, other_a, text_other_a)
    )
    other = join(other_a, other_b)
    second_other = weights_of(other, second, factor, offset)
    sum_second = shrunk(sum_second + dot_t(second_other, other))

    first_other_1 = weights_of(other_b[m:], first, factor, offset)
    late_other = shrunk(dot(first_other_1, first) + dot(second_other[q:], second))
    sum_second, late_other, second_own, second_other, first_other_1, sum_first, other_b = (
        lax.optimization_barrier(
            (sum_second, late_other, second_own, second_other, first_other_1, sum_first, other_b)
        )
    )
    got_late = swap(late_other, PC)
    got_a = swap(sum_second[:h], PY[1])
    got_b = swap(sum_second[h:], PX[1])
    first_own_1 = weights_of(own_1, first, factor, offset)
    late = dot(first_own_1, first) + dot(second_own[q:], second) + grown(got_late)
    late, first_own_1, first_other_1, text_own_0, text_other_a, second_own, second_other, sum_first, other_b = (
        lax.optimization_barrier(
            (
                shrunk(late),
                first_own_1,
                first_other_1,
                text_own_0,
                text_other_a,
                second_own,
                second_other,
                sum_first,
                other_b,
            )
        )
    )
    got_t = swap(late, PZ[1])

    first_other_0 = weights_of(other_b[:m], first, factor, offset)
    early_other = join(text_other_a, dot(first_other_0, first)) + dot(second_other[:q], second)
    got_early = swap(shrunk(early_other), PC)
    early = text_own_0 + dot(second_own[:q], second) + grown(got_early)
    sum_first = sum_first + dot_t(
        join(first_own_1, first_other_0, first_other_1), join(own_1, other_b)
    )

    ts = [early[i * m : (i + 1) * m] for i in range(3)]
    a, b = sum_first[:h], sum_first[h:]
    got_t, got_a, got_b = step(got_t, got_a, got_b)
    for k in (2, 1, 0):
        a, b = a + grown(got_a), b + grown(got_b)
        ts[k] = ts[k] + grown(got_t)
        q = a.shape[0] // 2
        out = ts[k] if k else ts[0][n:]
        got_a, got_b, got_t = step(
            swap(shrunk(a[q:]), (PX + PY)[k]),
            swap(shrunk(b[q:]), (PY + PX)[k]),
            swap(shrunk(out), PZ[k % 2]),
        )
        a, b = a[:q], b[:q]
    image_sum = join(a + grown(got_a), b + grown(got_b))
    return grads(images, texts, image_sum, ts[0][:n] + grown(got_t))


def solution(mesh):
    return jax.shard_map(
        body,
        mesh=mesh,
        in_specs=(P(("group", "blk"), None), P(("group", "blk"), None), P(), P()),
        out_specs=(P(("group", "blk"), None), P(("group", "blk"), None)),
        check_vma=False,
    )
```

```python
import jax
import jax.numpy as jnp
import numpy as np
from jax import lax
from jax.experimental import pallas as pl
from jax.experimental.pallas import tpu as pltpu
from jax.sharding import PartitionSpec as P

epsilon = 1e-06

SHAPE = (2, 2, 4, 2, 8)
AXES = ("group", "blk")
SHRINK = 0.25
SMALL = pltpu.CompilerParams(vmem_limit_bytes=4 * 2**20)


def pairs(axis, phase):
    partner = []
    for xh, core, y, xl, z in np.ndindex(*SHAPE):
        at = {"x": 2 * xh + xl, "y": y, "z": z}
        n = {"x": 4, "y": 4, "z": 8}[axis]
        p = at[axis]
        if (phase + core) % 2 == 0:
            at[axis] = p ^ 1
        else:
            at[axis] = (p + 1) % n if p % 2 else (p - 1) % n
        there = (at["x"] // 2, core, at["y"], at["x"] % 2, at["z"])
        partner.append(int(np.ravel_multi_index(there, SHAPE)))
    return partner


X0, X1, Y0, Y1 = pairs("x", 1), pairs("x", 0), pairs("y", 1), pairs("y", 0)
XY = [X0[i] for i in Y0]
Z0, Z1 = pairs("z", 0), pairs("z", 1)
ZFAR = [i ^ 4 for i in range(256)]
CORE = [i ^ 64 for i in range(256)]


def swap(array, partner):
    return lax.ppermute(array, AXES, list(enumerate(partner)))


def join(*arrays):
    return jnp.concatenate(arrays, axis=0)


def step(*arrays):
    return lax.optimization_barrier(arrays)


def unit_of(embedding):
    values = embedding.astype(jnp.float32)
    inverse = lax.rsqrt(jnp.sum(values * values, axis=-1, keepdims=True) + epsilon)
    return values * inverse, inverse


def low_kernel(texts, images, text_low, image_low):
    for rows, low in ((texts, text_low), (images, image_low)):
        low[...] = unit_of(rows[...])[0].astype(jnp.bfloat16)


def low_rows(texts, images):
    out = jax.ShapeDtypeStruct(texts.shape, jnp.bfloat16)
    return pl.pallas_call(low_kernel, out_shape=(out, out), compiler_params=SMALL)(texts, images)


def shrunk(part):
    return (part * SHRINK).astype(jnp.float16)


def grown(part):
    return part.astype(jnp.float32) * (1 / SHRINK)


def grads_kernel(images, texts, image_sum, text_sum, image_out, text_out):
    for rows, summed, out in ((images, image_sum, image_out), (texts, text_sum, text_out)):
        unit, inverse = unit_of(rows[...])
        total = summed[...]
        along = jnp.sum(unit * total, axis=-1, keepdims=True)
        out[...] = (total - unit * along) * inverse


def grads(images, texts, *sums):
    out = jax.ShapeDtypeStruct(images.shape, jnp.float32)
    return pl.pallas_call(grads_kernel, out_shape=(out, out), compiler_params=SMALL)(
        images, texts, *sums
    )


def weights_of(texts, images, factor, offset, own=None):
    product = lax.dot_general(
        texts, images, (((1,), (1,)), ((), ())), preferred_element_type=jnp.float32
    )
    value = jax.nn.sigmoid(factor * product + offset)
    if own is not None:
        row = lax.broadcasted_iota(jnp.int32, value.shape, 0)
        col = lax.broadcasted_iota(jnp.int32, value.shape, 1)
        value = value - ((row == col) & (row < own)).astype(jnp.float32)
    return (factor * value).astype(jnp.bfloat16)


def dot(a, b):
    return jnp.dot(a, b, preferred_element_type=jnp.float32)


def dot_t(a, b):
    return lax.dot_general(a, b, (((0,), (0,)), ((), ())), preferred_element_type=jnp.float32)


def body(images, texts, logit_scale, bias):
    factor = logit_scale[0]
    offset = bias[0]
    n = images.shape[0]
    text_low, image_low = low_rows(texts, images)

    t1, x1, y1, xy1 = step(
        swap(text_low, ZFAR), swap(image_low, X0), swap(image_low, Y0), swap(image_low, XY)
    )
    t, a, b = join(text_low, t1), join(image_low, x1), join(y1, xy1)
    got_t, got_a, got_b = step(swap(t, Z0), swap(a, X1), swap(b, Y1))
    own_a, a, b = join(t, got_t), join(a, got_a), join(b, got_b)
    first = join(a, b)
    got_a, got_b, own_b = step(swap(a, Y1), swap(b, X1), swap(own_a, Z1))

    first_own_a = weights_of(own_a, first, factor, offset, n)
    text_own_a = dot(first_own_a, first)
    sum_first = dot_t(first_own_a, own_a)

    h = 4 * n
    second = join(got_a, got_b)
    own = join(own_a, own_b)
    other = swap(own, CORE)
    second_own = weights_of(own, second, factor, offset)
    sum_second = dot_t(second_own, own)
    first_own_b = weights_of(own_b, first, factor, offset)
    text_own_b = dot(first_own_b, first)
    sum_second, second_own, text_own_b, other = lax.optimization_barrier(
        (sum_second, second_own, text_own_b, other)
    )
    second_other = weights_of(other, second, factor, offset)
    sum_second = shrunk(sum_second + dot_t(second_other, other))

    first_other_b = weights_of(other[h:], first, factor, offset)
    late_other = shrunk(dot(first_other_b, first) + dot(second_other[h:], second))
    sum_second, late_other, second_own, second_other, first_other_b, sum_first, other = (
        lax.optimization_barrier(
            (sum_second, late_other, second_own, second_other, first_other_b, sum_first, other)
        )
    )
    got_late = swap(late_other, CORE)
    got_a, got_b = swap(sum_second[:h], Y1), swap(sum_second[h:], X1)
    late = shrunk(text_own_b + dot(second_own[h:], second) + grown(got_late))
    late, first_own_b, first_other_b, text_own_a, other, second_own, second_other = (
        lax.optimization_barrier(
            (late, first_own_b, first_other_b, text_own_a, other, second_own, second_other)
        )
    )
    got_t = swap(late, Z1)

    first_other_a = weights_of(other[:h], first, factor, offset)
    text_other_a = dot(first_other_a, first)
    got_early = swap(shrunk(text_other_a + dot(second_other[:h], second)), CORE)
    t = text_own_a + dot(second_own[:h], second) + grown(got_early)
    sum_first = sum_first + dot_t(
        join(first_own_b, first_other_a, first_other_b), join(own_b, other)
    )

    got_a, got_b, got_t = step(got_a, got_b, got_t)
    a, b, t = sum_first[:h] + grown(got_a), sum_first[h:] + grown(got_b), t + grown(got_t)
    m = 2 * n
    got_a, got_b, got_t = step(
        swap(shrunk(a[m:]), X1), swap(shrunk(b[m:]), Y1), swap(shrunk(t[m:]), Z0)
    )
    a, b, t = a[:m] + grown(got_a), b[:m] + grown(got_b), t[:m] + grown(got_t)
    got_x, got_y, got_xy, got_t = step(
        swap(shrunk(a[n:]), X0),
        swap(shrunk(b[:n]), Y0),
        swap(shrunk(b[n:]), XY),
        swap(shrunk(t[n:]), ZFAR),
    )
    image_sum = a[:n] + grown(got_x) + grown(got_y) + grown(got_xy)
    return grads(images, texts, image_sum, t[:n] + grown(got_t))


def solution(mesh):
    return jax.shard_map(
        body,
        mesh=mesh,
        in_specs=(P(("group", "blk"), None), P(("group", "blk"), None), P(), P()),
        out_specs=(P(("group", "blk"), None), P(("group", "blk"), None)),
        check_vma=False,
    )
```

```python
import jax
import jax.numpy as jnp
import numpy as np
from jax import lax
from jax.experimental import pallas as pl
from jax.experimental.pallas import tpu as pltpu
from jax.sharding import PartitionSpec as P

epsilon = 1e-06

SHAPE = (2, 2, 4, 2, 8)
AXES = ("group", "blk")
SHRINK = 0.25
SMALL = pltpu.CompilerParams(vmem_limit_bytes=4 * 2**20)


def pairs(axis, phase):
    partner = []
    for xh, core, y, xl, z in np.ndindex(*SHAPE):
        at = {"x": 2 * xh + xl, "y": y, "z": z}
        n = {"x": 4, "y": 4, "z": 8}[axis]
        p = at[axis]
        if (phase + core) % 2 == 0:
            at[axis] = p ^ 1
        else:
            at[axis] = (p + 1) % n if p % 2 else (p - 1) % n
        there = (at["x"] // 2, core, at["y"], at["x"] % 2, at["z"])
        partner.append(int(np.ravel_multi_index(there, SHAPE)))
    return partner


X0, X1, Y0, Y1 = pairs("x", 1), pairs("x", 0), pairs("y", 1), pairs("y", 0)
XY = [X0[i] for i in Y0]
Z0, Z1 = pairs("z", 0), pairs("z", 1)
ZFAR = [i ^ 4 for i in range(256)]
CORE = [i ^ 64 for i in range(256)]


def swap(array, partner):
    return lax.ppermute(array, AXES, list(enumerate(partner)))


def join(*arrays):
    return jnp.concatenate(arrays, axis=0)


def step(*arrays):
    return lax.optimization_barrier(arrays)


def unit_of(embedding):
    values = embedding.astype(jnp.float32)
    inverse = lax.rsqrt(jnp.sum(values * values, axis=-1, keepdims=True) + epsilon)
    return values * inverse, inverse


def low_kernel(texts, images, text_low, image_low):
    for rows, low in ((texts, text_low), (images, image_low)):
        low[...] = unit_of(rows[...])[0].astype(jnp.bfloat16)


def low_rows(texts, images):
    out = jax.ShapeDtypeStruct(texts.shape, jnp.bfloat16)
    return pl.pallas_call(low_kernel, out_shape=(out, out), compiler_params=SMALL)(texts, images)


def shrunk(part):
    return (part * SHRINK).astype(jnp.float16)


def grown(part):
    return part.astype(jnp.float32) * (1 / SHRINK)


def grad_kernel(rows, summed, out):
    unit, inverse = unit_of(rows[...])
    total = summed[...]
    along = jnp.sum(unit * total, axis=-1, keepdims=True)
    out[...] = (total - unit * along) * inverse


def grad_rows(rows, summed):
    out = jax.ShapeDtypeStruct(rows.shape, jnp.float32)
    return pl.pallas_call(grad_kernel, out_shape=out, compiler_params=SMALL)(rows, summed)


def weights_of(texts, images, factor, offset, own=None):
    product = lax.dot_general(
        texts, images, (((1,), (1,)), ((), ())), preferred_element_type=jnp.float32
    )
    value = jax.nn.sigmoid(factor * product + offset)
    if own is not None:
        row = lax.broadcasted_iota(jnp.int32, value.shape, 0)
        col = lax.broadcasted_iota(jnp.int32, value.shape, 1)
        value = value - ((row == col) & (row < own)).astype(jnp.float32)
    return (factor * value).astype(jnp.bfloat16)


def dot(a, b):
    return jnp.dot(a, b, preferred_element_type=jnp.float32)


def dot_t(a, b):
    return lax.dot_general(a, b, (((0,), (0,)), ((), ())), preferred_element_type=jnp.float32)


def body(images, texts, logit_scale, bias):
    factor = logit_scale[0]
    offset = bias[0]
    n = images.shape[0]
    text_low, image_low = low_rows(texts, images)

    t1 = swap(text_low, ZFAR)
    x1, y1, xy1 = step(swap(image_low, X0), swap(image_low, Y0), swap(image_low, XY))
    t, a, b = join(text_low, t1), join(image_low, x1), join(y1, xy1)
    got_t, got_a, got_b = swap(t, Z0), swap(a, X1), swap(b, Y1)
    own_a, a, b = join(t, got_t), join(a, got_a), join(b, got_b)
    first = join(a, b)
    got_a, got_b, own_b = swap(a, Y1), swap(b, X1), swap(own_a, Z1)

    first_own_a = weights_of(own_a, first, factor, offset, n)
    text_own_a = dot(first_own_a, first)
    sum_first = dot_t(first_own_a, own_a)

    h = 4 * n
    second = join(got_a, got_b)
    own = join(own_a, own_b)
    other = swap(own, CORE)
    second_own = weights_of(own, second, factor, offset)
    sum_second = dot_t(second_own, own)
    first_own_b = weights_of(own_b, first, factor, offset)
    text_own_b = dot(first_own_b, first)
    sum_second, second_own, text_own_b, other = lax.optimization_barrier(
        (sum_second, second_own, text_own_b, other)
    )
    second_other = weights_of(other, second, factor, offset)
    sum_second = shrunk(sum_second + dot_t(second_other, other))

    first_other_b = weights_of(other[h:], first, factor, offset)
    late_other = shrunk(dot(first_other_b, first) + dot(second_other[h:], second))
    sum_second, late_other, second_own, second_other, first_other_b, sum_first, other = (
        lax.optimization_barrier(
            (sum_second, late_other, second_own, second_other, first_other_b, sum_first, other)
        )
    )
    got_late = swap(late_other, CORE)
    got_a, got_b = swap(sum_second[:h], Y1), swap(sum_second[h:], X1)
    late = shrunk(text_own_b + dot(second_own[h:], second) + grown(got_late))
    late, first_own_b, first_other_b, text_own_a, other, second_own, second_other = (
        lax.optimization_barrier(
            (late, first_own_b, first_other_b, text_own_a, other, second_own, second_other)
        )
    )
    got_t = swap(late, Z1)

    first_other_a = weights_of(other[:h], first, factor, offset)
    text_other_a = dot(first_other_a, first)
    got_early = swap(shrunk(text_other_a + dot(second_other[:h], second)), CORE)
    t = text_own_a + dot(second_own[:h], second) + grown(got_early)
    sum_first = sum_first + dot_t(
        join(first_own_b, first_other_a, first_other_b), join(own_b, other)
    )

    got_a, got_b, got_t = step(got_a, got_b, got_t)
    a, b, t = sum_first[:h] + grown(got_a), sum_first[h:] + grown(got_b), t + grown(got_t)
    m = 2 * n
    got_a, got_b = step(swap(shrunk(a[m:]), X1), swap(shrunk(b[m:]), Y1))
    got_t = swap(shrunk(t[m:]), Z0)
    a, b, t = a[:m] + grown(got_a), b[:m] + grown(got_b), t[:m] + grown(got_t)
    got_b, got_t = swap(shrunk(b), Y0), swap(shrunk(t[n:]), ZFAR)
    a = a + grown(got_b)
    image_sum = a[:n] + grown(swap(shrunk(a[n:]), X0))
    return grad_rows(images, image_sum), grad_rows(texts, t[:n] + grown(got_t))


def solution(mesh):
    return jax.shard_map(
        body,
        mesh=mesh,
        in_specs=(P(("group", "blk"), None), P(("group", "blk"), None), P(), P()),
        out_specs=(P(("group", "blk"), None), P(("group", "blk"), None)),
        check_vma=False,
    )
```

```python
import jax
import jax.numpy as jnp
import numpy as np
from jax import lax
from jax.experimental import pallas as pl
from jax.experimental.pallas import tpu as pltpu
from jax.sharding import PartitionSpec as P

epsilon = 1e-06

SHAPE = (2, 2, 4, 2, 8)
AXES = ("group", "blk")
SHRINK = 0.25
SMALL = pltpu.CompilerParams(vmem_limit_bytes=4 * 2**20)


def pairs(axis, phase):
    partner = []
    for xh, core, y, xl, z in np.ndindex(*SHAPE):
        at = {"x": 2 * xh + xl, "y": y, "z": z}
        n = {"x": 4, "y": 4, "z": 8}[axis]
        p = at[axis]
        if (phase + core) % 2 == 0:
            at[axis] = p ^ 1
        else:
            at[axis] = (p + 1) % n if p % 2 else (p - 1) % n
        there = (at["x"] // 2, core, at["y"], at["x"] % 2, at["z"])
        partner.append(int(np.ravel_multi_index(there, SHAPE)))
    return partner


X0, X1, Y0, Y1 = pairs("x", 1), pairs("x", 0), pairs("y", 1), pairs("y", 0)
XY = [X0[i] for i in Y0]
Z0, Z1 = pairs("z", 0), pairs("z", 1)
ZFAR = [i ^ 4 for i in range(256)]
CORE = [i ^ 64 for i in range(256)]


def swap(array, partner):
    return lax.ppermute(array, AXES, list(enumerate(partner)))


def join(*arrays):
    return jnp.concatenate(arrays, axis=0)


def step(*arrays):
    return lax.optimization_barrier(arrays)


def unit_of(embedding):
    values = embedding.astype(jnp.float32)
    inverse = lax.rsqrt(jnp.sum(values * values, axis=-1, keepdims=True) + epsilon)
    return values * inverse, inverse


def low_kernel(texts, images, text_low, image_low):
    for rows, low in ((texts, text_low), (images, image_low)):
        low[...] = unit_of(rows[...])[0].astype(jnp.bfloat16)


def low_rows(texts, images):
    out = jax.ShapeDtypeStruct(texts.shape, jnp.bfloat16)
    return pl.pallas_call(low_kernel, out_shape=(out, out), compiler_params=SMALL)(texts, images)


def shrunk(part):
    return (part * SHRINK).astype(jnp.float16)


def grown(part):
    return part.astype(jnp.float32) * (1 / SHRINK)


def grad_kernel(rows, summed, out):
    unit, inverse = unit_of(rows[...])
    total = summed[...]
    along = jnp.sum(unit * total, axis=-1, keepdims=True)
    out[...] = (total - unit * along) * inverse


def grad_rows(rows, summed):
    out = jax.ShapeDtypeStruct(rows.shape, jnp.float32)
    return pl.pallas_call(grad_kernel, out_shape=out, compiler_params=SMALL)(rows, summed)


def weights_of(texts, images, factor, offset, own=None):
    product = lax.dot_general(
        texts, images, (((1,), (1,)), ((), ())), preferred_element_type=jnp.float32
    )
    value = jax.nn.sigmoid(factor * product + offset)
    if own is not None:
        row = lax.broadcasted_iota(jnp.int32, value.shape, 0)
        col = lax.broadcasted_iota(jnp.int32, value.shape, 1)
        value = value - ((row == col) & (row < own)).astype(jnp.float32)
    return (factor * value).astype(jnp.bfloat16)


def dot(a, b):
    return jnp.dot(a, b, preferred_element_type=jnp.float32)


def dot_t(a, b):
    return lax.dot_general(a, b, (((0,), (0,)), ((), ())), preferred_element_type=jnp.float32)


def body(images, texts, logit_scale, bias):
    factor = logit_scale[0]
    offset = bias[0]
    n = images.shape[0]
    text_low, image_low = low_rows(texts, images)

    t1 = swap(text_low, ZFAR)
    x1, y1, xy1 = step(swap(image_low, X0), swap(image_low, Y0), swap(image_low, XY))
    t, a, b = join(text_low, t1), join(image_low, x1), join(y1, xy1)
    got_a, got_b, got_t = swap(a, X1), swap(b, Y1), swap(t, Z0)
    own_a, a, b = join(t, got_t), join(a, got_a), join(b, got_b)
    first = join(a, b)
    got_a, got_b, own_b = swap(a, Y1), swap(b, X1), swap(own_a, Z1)

    first_own_a = weights_of(own_a, first, factor, offset, n)
    text_own_a = dot(first_own_a, first)
    sum_first = dot_t(first_own_a, own_a)

    h = 4 * n
    second = join(got_a, got_b)
    own = join(own_a, own_b)
    other = swap(own, CORE)
    second_own = weights_of(own, second, factor, offset)
    sum_second = dot_t(second_own, own)
    first_own_b = weights_of(own_b, first, factor, offset)
    text_own_b = dot(first_own_b, first)
    sum_second, second_own, text_own_b, other = lax.optimization_barrier(
        (sum_second, second_own, text_own_b, other)
    )
    second_other = weights_of(other, second, factor, offset)
    sum_second = shrunk(sum_second + dot_t(second_other, other))

    first_other_b = weights_of(other[h:], first, factor, offset)
    late_other = shrunk(dot(first_other_b, first) + dot(second_other[h:], second))
    sum_second, late_other, second_own, second_other, first_other_b, sum_first, other = (
        lax.optimization_barrier(
            (sum_second, late_other, second_own, second_other, first_other_b, sum_first, other)
        )
    )
    got_late = swap(late_other, CORE)
    got_a, got_b = swap(sum_second[:h], Y1), swap(sum_second[h:], X1)
    late = shrunk(text_own_b + dot(second_own[h:], second) + grown(got_late))
    late, first_own_b, first_other_b, text_own_a, other, second_own, second_other = (
        lax.optimization_barrier(
            (late, first_own_b, first_other_b, text_own_a, other, second_own, second_other)
        )
    )
    got_t = swap(late, Z1)

    first_other_a = weights_of(other[:h], first, factor, offset)
    text_other_a = dot(first_other_a, first)
    got_early = swap(shrunk(text_other_a + dot(second_other[:h], second)), CORE)
    t = text_own_a + dot(second_own[:h], second) + grown(got_early)
    sum_first = sum_first + dot_t(
        join(first_own_b, first_other_a, first_other_b), join(own_b, other)
    )

    got_a, got_t = step(got_a, got_t)
    a, b, t = sum_first[:h] + grown(got_a), sum_first[h:] + grown(got_b), t + grown(got_t)
    m = 2 * n
    got_a, got_b = step(swap(shrunk(a[m:]), X1), swap(shrunk(b[m:]), Y1))
    got_t = swap(shrunk(t[m:]), Z0)
    a, b, t = a[:m] + grown(got_a), b[:m] + grown(got_b), t[:m] + grown(got_t)
    got_b, got_t = swap(shrunk(b), Y0), swap(shrunk(t[n:]), ZFAR)
    a = a + grown(got_b)
    image_sum = a[:n] + grown(swap(shrunk(a[n:]), X0))
    return grad_rows(images, image_sum), grad_rows(texts, t[:n] + grown(got_t))


def solution(mesh):
    return jax.shard_map(
        body,
        mesh=mesh,
        in_specs=(P(("group", "blk"), None), P(("group", "blk"), None), P(), P()),
        out_specs=(P(("group", "blk"), None), P(("group", "blk"), None)),
        check_vma=False,
    )
```
